512 devices in a mesh: rows: 64 (over x, z), cols: 8 (over y, core).
Axes of the slice: x: 4, y: 4, z: 16, core: 2. Of those that a mesh axis runs over, the one named last changes fastest.
Arguments:
- right_side: float32 [16, 32768], P(None, 'rows'), may hold values from -6 to 6
- child_updates: float32 [16384, 16, 128], P('rows', 'cols'), may hold values from -6 to 6
- child_device: int32 [16384, 1], P('rows'), may hold values from 0 to 63; in each aligned block of 256 rows (0 to 255, 256 to 511, ...) at most 8 rows name the same one
- child_block: int32 [16384, 1], P('rows'), may hold values from 0 to 3
- owners: int32 [2], replicated, may hold values from 0 to 63, as said below
- diag_inverse: bfloat16 [2, 512, 512], P(None, 'cols'), may hold values from -0.25 to 0.25
- panel_factor: bfloat16 [2, 512, 32768], P(None, 'cols', 'rows'), may hold values from -0.25 to 0.25
Outputs:
- front_state: float32 [16, 32768], P(None, 'rows')
The draws below stay inside these ranges and needn't reach their ends.
Inputs may be any that keep to these rules, and one draw needn't show every extreme that they name: `child_device`: among the child blocks of one rows index (aligned blocks of 256 rows) no panel is named more than 8 times. `owners`: the entries are distinct.
All inputs are finite; a program needn't handle non-finite values.
Results may differ from the reference program's by a relative error of at most 0.0003.
Values sent between devices are 32-bit elements; how exact they have to be, the bound alone decides.
A program may use at most 64 MiB of HBM per device.

```python
import math
import jax
import jax.numpy as jnp
import numpy as np
from jax import lax

K = 16
PANEL = 512
BLK = 128
NPAN = 2
NB_DEV = 256
CAP = 8
FRONT = 32768
NBLK = 16384
N_ROWS = 64


def draw_owners(key, part):
    key = jax.random.fold_in(key, 7)
    order_key, place_key = jax.random.split(key)
    order = jax.random.permutation(order_key, N_ROWS).astype(jnp.int32)
    where_top = jnp.argmax((order == N_ROWS - 1).astype(jnp.int32)).astype(jnp.int32)
    place = jax.random.randint(place_key, (), 0, NPAN).astype(jnp.int32)
    moved = order[place]
    order = order.at[where_top].set(moved).at[place].set(jnp.int32(N_ROWS - 1))
    return order[:NPAN].astype(jnp.int32)


def touch_ends(array, key, smallest, high):
    spot = [jax.random.randint(jax.random.fold_in(key, axis), (), 0, length) for axis, length in enumerate(array.shape)]
    widest = array.shape.index(max(array.shape))
    beside = spot[:widest] + [(spot[widest] + 1) % array.shape[widest]] + spot[widest + 1:]
    return array.at[tuple(spot)].set(smallest).at[tuple(beside)].set(high)


def block_levels(rng, shape, cuts, least, high):
    level, own = 1.0, jax.random.fold_in(rng, 6)
    for position, shards_of in cuts:
        draws = jnp.exp(jax.random.uniform(jax.random.fold_in(own, position), (shards_of,), jnp.float32, least / len(cuts), high / len(cuts)))
        level = level * jnp.repeat(draws, shape[position] // shards_of).reshape([-1 if axis == position else 1 for axis in range(len(shape))])
    return level


def assign_block(rng, own, number, rows, count, top, limit, slope):
    sequence = jax.random.permutation(rng, count)
    packed, common = shares(count, rows * top, limit, slope, True), shares(count, rows * top, limit, slope, False)
    places = jnp.arange(count)

    def named(sizes, turn):
        used = int((sizes > 0).sum())
        fixed = max(1, used // 4)
        moved = fixed + (places - fixed + turn * (used - fixed)) % max(1, count - fixed)
        return jnp.zeros((count,), jnp.int32).at[sequence[jnp.where(places < fixed, places, moved)]].set(jnp.asarray(sizes, jnp.int32))

    sizes = jnp.where(number % 4 == 0, named(packed, number // 4), named(common, number - number // 4 - 1))
    mixed = jax.random.permutation(jax.random.fold_in(own, 3), count)
    source_of, receiver = mixed[0:count // 2 * 2:2], mixed[1:count // 2 * 2:2]
    slack = jnp.minimum(sizes[source_of] - 1, limit - sizes[receiver]) // 2
    slack = jnp.where((source_of == sequence[0]) | (receiver == sequence[0]) | (sizes[receiver] == 0), 0, jnp.maximum(slack, 0))
    moved = jax.random.randint(jax.random.fold_in(own, 4), (count // 2,), 0, 1 << 20) % (slack + 1)
    sizes = sizes.at[source_of].add(-moved).at[receiver].add(moved)
    items = jnp.searchsorted(jnp.cumsum(sizes), jnp.arange(rows * top), side="right").astype(jnp.int32)
    grid = items.reshape(top, rows).T
    grid = grid[jax.random.permutation(jax.random.fold_in(own, 1), rows)]
    turn = jax.random.randint(jax.random.fold_in(own, 2), (rows, 1), 0, top)
    return jnp.take_along_axis(grid, (jnp.arange(top)[None, :] + turn) % top, axis=1)


def shares(amount, total, reach, slope, full):
    weights = [(1 << 20) // math.isqrt(grade ** slope) + 1 for grade in range(1, amount + 1)]
    largest = reach if full else min(reach, max(-(-total // amount), total * weights[0] // sum(weights)))
    least = 1 if total - largest >= amount - 1 else 0
    holding, surplus = [largest] + [least] * (amount - 1), total - largest - least * (amount - 1)
    while surplus > 0:
        free = [i for i in range(1, amount) if holding[i] < largest] or [i for i in range(1, amount) if holding[i] < reach]
        whole, remaining = sum([weights[i] for i in free]), surplus
        for i in free:
            addition = min(reach - holding[i], max(1, remaining * weights[i] // whole), surplus)
            holding[i] = holding[i] + addition
            surplus = surplus - addition
    return np.array(holding)


def normal_values(own_key, dims, width, limit, cuts=(), kind=jnp.bfloat16):
    entries = width * jax.random.normal(own_key, dims, jnp.float32)
    if cuts:
        entries = entries * block_levels(own_key, dims, cuts, -0.22, 0.18)
    return jnp.clip(entries, -limit, limit).astype(kind)


def setup_inputs(seed: int = 0) -> dict:
    key_list = jax.random.split(jax.random.key(seed), 8)
    right_side = normal_values(key_list[0], (K, FRONT), 1.0, 6.0, ((1, 64),), jnp.float32)
    child_updates = normal_values(key_list[1], (NBLK, K, BLK), 1.0, 6.0, ((0, 64), (1, 8)), jnp.float32)
    child_device_keys = jax.random.split(jax.random.fold_in(key_list[2], 1), NBLK // NB_DEV)
    child_device_turns = jax.random.permutation(jax.random.fold_in(key_list[2], 3), NBLK // NB_DEV)
    child_device = jax.vmap(lambda own, number: assign_block(jax.random.fold_in(key_list[2], 2), own, number, NB_DEV, N_ROWS, 1, CAP, 2))(child_device_keys, child_device_turns).reshape((NBLK, 1))
    child_block = touch_ends(jax.random.randint(key_list[3], (NBLK, 1), 0, PANEL // BLK), jax.random.fold_in(key_list[3], 1), 0, (PANEL // BLK) - 1).astype(jnp.int32)
    owners = draw_owners(jax.random.fold_in(key_list[7], 71), 0)
    diag_inverse = normal_values(key_list[5], (NPAN, PANEL, PANEL), PANEL ** -0.5, 0.25, ((1, 8),))
    panel_factor = normal_values(key_list[6], (NPAN, PANEL, FRONT), PANEL ** -0.5, 0.25, ((1, 8), (2, 64)))
    return dict(right_side=right_side, child_updates=child_updates, child_device=child_device, child_block=child_block, owners=owners, diag_inverse=diag_inverse, panel_factor=panel_factor)


def reference(right_side, child_updates, child_device, child_block, owners, diag_inverse, panel_factor):
    per_panel = PANEL // BLK
    target = (child_device[:, 0] * per_panel + child_block[:, 0]).astype(jnp.int32)
    summed = jax.ops.segment_sum(child_updates, target, num_segments=N_ROWS * per_panel)
    assembled = jnp.transpose(summed, (1, 0, 2)).reshape(K, N_ROWS * PANEL)
    state = right_side + assembled
    panel_of = (jnp.arange(N_ROWS * PANEL, dtype=jnp.int32) // PANEL).astype(jnp.int32)
    for step in range(NPAN):
        root = owners[step].astype(jnp.int32)
        start = (root * PANEL).astype(jnp.int32)
        side = lax.dynamic_slice_in_dim(state, start, PANEL, 1)
        solution = jnp.dot(side, diag_inverse[step].astype(jnp.float32).T, precision=lax.Precision.HIGHEST)
        update = jnp.dot(solution, panel_factor[step].astype(jnp.float32), precision=lax.Precision.HIGHEST)
        done = jnp.any(panel_of[:, None] == owners[None, :step + 1], axis=1)
        state = jnp.where(done[None, :], state, state - update)
        state = lax.dynamic_update_slice_in_dim(state, solution, start, 1)
    return state
```

```python
import functools

import jax
import jax.numpy as jnp
from jax import lax
from jax.experimental import pallas as pl
from jax.experimental.pallas import tpu as pltpu
from jax.sharding import PartitionSpec as P

MESH = pl.DeviceIdType.MESH
F32, BF16 = jnp.float32, jnp.bfloat16
NX, NY, NC, NZ = 4, 4, 2, 16

Z_OFFS = (8, 7, 9, 6, 10, 5, 11, 4, 12, 3, 13, 2, 14, 1, 15)
X_OFFS = (2, 1, 3)
C_OFFS = tuple((dy, dk) for dy in (2, 1, 3, 0) for dk in (0, 1) if dy or dk)
XC_OFFS = tuple((dx, dy, dk) for dx in (2, 1, 3, 0) for dy in (2, 1, 3, 0) for dk in (0, 1) if dx or dy or dk)


def split(value):
    high = value.astype(BF16)
    return high, (value - high.astype(F32)).astype(BF16)


def stacked(value):
    return jnp.concatenate(split(value), axis=0)


def folded(value):
    half = value.shape[0] // 2
    return value[:half] + value[half:]


def dot(a, b):
    return jnp.dot(a, b, preferred_element_type=F32)


def dot_t(a, b):
    return lax.dot_general(a, b, (((1,), (1,)), ((), ())), preferred_element_type=F32)


def kernel(
    owners, right, child, dev, blk, diag, fac, out,
    summed, fmask, fz, fmine, fx, pown, pz, pmine, px, dmine, dg, mx, mmine, mz, tz, part, pr, xs, rown, order, send, recv,
):
    row, col = lax.axis_index("rows"), lax.axis_index("cols")
    x, z, y, k = row // NZ, row % NZ, col // NC, col % NC

    def z_peer(d):
        return (x * NZ + (z + d) % NZ, col)

    def x_peer(d):
        return ((x + d) % NX * NZ + z, col)

    def c_peer(d):
        return (row, (y + d[0]) % NY * NC + (k + d[1]) % NC)

    def xc_peer(d):
        return ((x + d[0]) % NX * NZ + z, (y + d[1]) % NY * NC + (k + d[2]) % NC)

    barrier = pltpu.get_barrier_semaphore()
    peers = [z_peer(d) for d in Z_OFFS] + [xc_peer(d) for d in XC_OFFS]
    for peer in peers:
        pl.semaphore_signal(barrier, inc=1, device_id=peer, device_id_type=MESH)

    def put(group, src, dst, peer):
        pltpu.make_async_remote_copy(src, dst, send.at[group], recv.at[group], device_id=peer, device_id_type=MESH).start()

    def whole(group, ref):
        return pltpu.make_async_remote_copy(
            ref, ref, send.at[group], recv.at[group], device_id=x_peer(1), device_id_type=MESH
        )

    first, second = owners[0], owners[1]
    is_first = (row == first).astype(F32)
    is_second = (row == second).astype(F32)
    other = (1.0 - is_first) * (1.0 - is_second)

    block = fac[0].astype(F32) * is_second
    for ig in range(4):
        for jb in range(4):
            fmask[ig * 4 + jb] = block[ig * 16:ig * 16 + 16, jb * 128:jb * 128 + 128]
    ig = z // 4
    dmine[...] = diag[0, pl.ds(pl.multiple_of(ig * 16, 16), 16), :].astype(F32)

    place = dev[...] * 8 + blk[...]
    rows = lax.broadcasted_iota(jnp.int32, (512, 256), 0)
    hot = jnp.concatenate([(rows == place).astype(F32).astype(BF16), (rows == place + 4).astype(F32).astype(BF16)], axis=1)
    upper = jnp.concatenate(split(child[:, 0, :]), axis=1)
    lower = jnp.concatenate(split(child[:, 1, :]), axis=1)
    total = dot(hot, jnp.concatenate([upper, lower], axis=0))
    summed[...] = (total[:, :128] + total[:, 128:]).reshape(64, 8, 128)

    chosen = lax.broadcasted_iota(jnp.int32, (8, 128), 0) == col
    for b in range(4):
        order[b] = right[:, b * 128:b * 128 + 128]
        for kk in range(2):
            lines = jnp.where(chosen, order[b, pl.ds(kk, 8, stride=2), :], 0.0)
            rown[kk * 4 + b:kk * 4 + b + 1, :] = jnp.sum(lines, axis=0, keepdims=True)
    pown[0] = summed[first] + rown[...] * is_first
    pown[1] = summed[second] + rown[...] * is_second

    pl.semaphore_wait(barrier, len(peers))

    for s, d in enumerate(Z_OFFS):
        put(0, pown.at[0], pz.at[0, s], z_peer(d))
    for s, d in enumerate(Z_OFFS):
        put(2, fmask.at[(z + d) % NZ], fz.at[s], z_peer(d))
    for s, d in enumerate(Z_OFFS):
        put(1, pown.at[1], pz.at[1, s], z_peer(d))
    for d in C_OFFS:
        put(3, dmine, dg.at[col], c_peer(d))
    dg[col] = dmine[...]
    for s, d in enumerate(X_OFFS):
        put(4, summed.at[pl.ds((x + d) % NX * NZ, NZ)], mx.at[s], x_peer(d))

    def panel_sum(p):
        whole(p, pz.at[p]).wait_recv()
        pmine[p] = pown[p] + jnp.sum(pz[p], axis=0)
        for d in XC_OFFS:
            put(5 + p, pmine.at[p], px.at[p, (4 - d[0]) % 4 * 8 + col], xc_peer(d))
        px[p, col] = pmine[p]

    panel_sum(0)
    whole(2, fz).wait_recv()
    fmine[...] = fmask[z] + jnp.sum(fz[...], axis=0)
    for d in XC_OFFS:
        put(7, fmine, fx.at[(4 - d[0]) % 4 * 8 + col], xc_peer(d))
    fx[col] = fmine[...]
    panel_sum(1)
    whole(4, mx).wait_recv()
    mmine[...] = summed[pl.ds(x * NZ, NZ)] + mx[0] + mx[1] + mx[2]
    for s, d in enumerate(Z_OFFS):
        put(8, mmine.at[(z + d) % NZ], mz.at[s], z_peer(d))

    def panel_state(p):
        whole(5 + p, px.at[p, pl.ds(0, 31)]).wait_recv()
        value = px[p, 0:8] + px[p, 8:16] + px[p, 16:24] + px[p, 24:32]
        xs[p] = value.reshape(64, 128)
        return jnp.concatenate(
            [jnp.concatenate([xs[p, pl.ds(kk * 4 + b, 8, stride=8), :] for kk in range(2)], axis=0) for b in range(4)],
            axis=1,
        )

    eye = (
        lax.broadcasted_iota(jnp.int32, (64, 512), 1) == lax.broadcasted_iota(jnp.int32, (64, 512), 0) + col * 64
    ).astype(F32)
    w_first = (eye * is_first - fac[0].astype(F32) * other).astype(BF16)
    w_second = (eye * is_second - fac[1].astype(F32) * (1.0 - is_second) * (1.0 - is_first)).astype(BF16)

    state = stacked(panel_state(0))
    whole(3, dg.at[pl.ds(0, 7)]).wait_recv()
    group = folded(dot_t(state, dg[...].reshape(128, 512).astype(BF16)))
    whole(7, fx.at[pl.ds(0, 31)]).wait_recv()
    piece = (fx[0:8] + fx[8:16] + fx[16:24] + fx[24:32]).reshape(128, 128).astype(BF16)
    tz[z] = folded(dot(stacked(group), piece))
    for d in Z_OFFS:
        put(9, tz.at[z], tz.at[z], z_peer(d))

    solved = folded(dot_t(state, diag[0]))
    partial = folded(dot(stacked(solved), w_first))
    whole(8, mz).wait_recv()
    assembled = (mmine[z] + jnp.sum(mz[...], axis=0)) * other
    mine = lax.broadcasted_iota(jnp.int32, (8, 128), 0) == col
    placed = jnp.concatenate(
        [
            jnp.concatenate(
                [jnp.where(mine, assembled[kk * 4 + b:kk * 4 + b + 1, :], 0.0) for kk in range(2)], axis=0
            )
            for b in range(4)
        ],
        axis=1,
    )
    partial = partial + placed
    state = panel_state(1)

    whole(9, tz.at[pl.ds(0, 15)]).wait_recv()
    update = jnp.concatenate([tz[b] + tz[4 + b] + tz[8 + b] + tz[12 + b] for b in range(4)], axis=1)
    solved = folded(dot_t(stacked(state - update), diag[1]))
    part[...] = partial + folded(dot(stacked(solved), w_second))
    for s, d in enumerate(C_OFFS):
        put(10, part, pr.at[s], c_peer(d))
    whole(10, pr).wait_recv()
    total = part[...] + jnp.sum(pr[...], axis=0)
    for b in range(4):
        for kk in range(2):
            order[b, pl.ds(kk, 8, stride=2), :] = total[kk * 8:kk * 8 + 8, b * 128:b * 128 + 128]
        lanes = slice(b * 128, b * 128 + 128)
        out[:, lanes] = order[b] + right[:, lanes] * other

    whole(0, pz.at[0]).wait_send()
    whole(1, pz.at[1]).wait_send()
    whole(2, fz).wait_send()
    whole(3, dg.at[pl.ds(0, 7)]).wait_send()
    whole(4, mx).wait_send()
    whole(5, px.at[0, pl.ds(0, 31)]).wait_send()
    whole(6, px.at[1, pl.ds(0, 31)]).wait_send()
    whole(7, fx.at[pl.ds(0, 31)]).wait_send()
    whole(8, mz).wait_send()
    whole(9, tz.at[pl.ds(0, 15)]).wait_send()
    whole(10, pr).wait_send()


def body(right_side, child_updates, child_device, child_block, owners, diag_inverse, panel_factor):
    vmem = pl.BlockSpec(memory_space=pltpu.VMEM)
    return pl.pallas_call(
        kernel,
        out_shape=jax.ShapeDtypeStruct((16, 512), F32),
        in_specs=[pl.BlockSpec(memory_space=pltpu.SMEM)] + [vmem] * 6,
        out_specs=vmem,
        scratch_shapes=[
            pltpu.VMEM((64, 8, 128), F32),
            pltpu.VMEM((16, 16, 128), F32),
            pltpu.VMEM((15, 16, 128), F32),
            pltpu.VMEM((16, 128), F32),
            pltpu.VMEM((32, 16, 128), F32),
            pltpu.VMEM((2, 8, 128), F32),
            pltpu.VMEM((2, 15, 8, 128), F32),
            pltpu.VMEM((2, 8, 128), F32),
            pltpu.VMEM((2, 32, 8, 128), F32),
            pltpu.VMEM((16, 512), F32),
            pltpu.VMEM((8, 16, 512), F32),
            pltpu.VMEM((3, 16, 8, 128), F32),
            pltpu.VMEM((16, 8, 128), F32),
            pltpu.VMEM((15, 8, 128), F32),
            pltpu.VMEM((16, 16, 128), F32),
            pltpu.VMEM((16, 512), F32),
            pltpu.VMEM((7, 16, 512), F32),
            pltpu.VMEM((2, 64, 128), F32),
            pltpu.VMEM((8, 128), F32),
            pltpu.VMEM((4, 16, 128), F32),
            pltpu.SemaphoreType.DMA((11,)),
            pltpu.SemaphoreType.DMA((11,)),
        ],
        compiler_params=pltpu.CompilerParams(
            collective_id=0, has_side_effects=True, vmem_limit_bytes=32 * 1024 * 1024
        ),
    )(
        owners, right_side, child_updates, child_device.reshape(1, 256), child_block.reshape(1, 256),
        diag_inverse, panel_factor,
    )


def solution(mesh):
    return jax.shard_map(
        body,
        mesh=mesh,
        in_specs=(
            P(None, "rows"),
            P("rows", "cols", None),
            P("rows", None),
            P("rows", None),
            P(),
            P(None, "cols", None),
            P(None, "cols", "rows"),
        ),
        out_specs=P(None, "rows"),
        check_vma=False,
    )
```

```python
import functools

import jax
import jax.numpy as jnp
from jax import lax
from jax.experimental import pallas as pl
from jax.experimental.pallas import tpu as pltpu
from jax.sharding import PartitionSpec as P

MESH = pl.DeviceIdType.MESH
F32, BF16 = jnp.float32, jnp.bfloat16
NX, NY, NC, NZ = 4, 4, 2, 16

NEAR = (4, -4, 3, -3, 2, -2, 1, -1)
Z_OFFS = (8, 7, 9, 6, 10, 5, 11, 4, 12, 3, 13, 2, 14, 1, 15)
X_OFFS = (2, 1, 3)
C_OFFS = tuple((dy, dk) for dy in (2, 1, 3, 0) for dk in (0, 1) if dy or dk)
XC_OFFS = tuple((dx, dy, dk) for dx in (2, 1, 3, 0) for dy in (2, 1, 3, 0) for dk in (0, 1) if dx or dy or dk)


def split(value):
    high = value.astype(BF16)
    return high, (value - high.astype(F32)).astype(BF16)


def stacked(value):
    return jnp.concatenate(split(value), axis=0)


def folded(value):
    half = value.shape[0] // 2
    return value[:half] + value[half:]


def dot(a, b):
    return jnp.dot(a, b, preferred_element_type=F32)


def dot_t(a, b):
    return lax.dot_general(a, b, (((1,), (1,)), ((), ())), preferred_element_type=F32)


def kernel(
    owners_any, right_any, child_any, dev_any, blk_any, diag_any, fac_any, out,
    owners, right, child, dev, blk, diag, fac, local,
    summed, fmask, fz, fmine, fx, pown, pz, pmine, px, dmine, dg, mx, mmine, mz, tz, part, pr, xs, rown, order, dfull, ffull, dhalf, fhalf, pside, pfar, frelay, fpass, send, recv,
):
    row, col = lax.axis_index("rows"), lax.axis_index("cols")
    x, z, y, k = row // NZ, row % NZ, col // NC, col % NC

    def z_peer(d):
        return (x * NZ + (z + d + NZ) % NZ, col)

    def x_peer(d):
        return ((x + d) % NX * NZ + z, col)

    def c_peer(d):
        return (row, (y + d[0]) % NY * NC + (k + d[1]) % NC)

    def xc_peer(d):
        return ((x + d[0]) % NX * NZ + z, (y + d[1]) % NY * NC + (k + d[2]) % NC)

    loads = [
        pltpu.make_async_copy(src, dst, local.at[i])
        for i, (src, dst) in enumerate(
            [
                (owners_any, owners), (fac_any.at[0], fac.at[0]), (dev_any, dev), (blk_any, blk), (child_any, child),
                (right_any, right), (diag_any, diag), (fac_any.at[1], fac.at[1]),
            ]
        )
    ]
    for load in loads:
        load.start()

    barrier = pltpu.get_barrier_semaphore()
    peers = [z_peer(d) for d in NEAR] + [xc_peer(d) for d in XC_OFFS]
    for peer in peers:
        pl.semaphore_signal(barrier, inc=1, device_id=peer, device_id_type=MESH)

    def put(group, src, dst, peer):
        pltpu.make_async_remote_copy(src, dst, send.at[group], recv.at[group], device_id=peer, device_id_type=MESH).start()

    def whole(group, ref):
        return pltpu.make_async_remote_copy(
            ref, ref, send.at[group], recv.at[group], device_id=x_peer(1), device_id_type=MESH
        )

    loads[0].wait()
    first, second = owners[0], owners[1]
    is_first = (row == first).astype(F32)
    is_second = (row == second).astype(F32)
    other = (1.0 - is_first) * (1.0 - is_second)

    loads[1].wait()
    block = fac[0].astype(F32) * is_second
    for ig in range(4):
        for jb in range(4):
            fmask[(ig * 4 + jb - z + NZ) % NZ] = block[ig * 16:ig * 16 + 16, jb * 128:jb * 128 + 128]
    loads[2].wait()
    loads[3].wait()
    place = dev[...] * 8 + blk[...]
    rows = lax.broadcasted_iota(jnp.int32, (512, 256), 0)
    hot = jnp.concatenate([(rows == place).astype(F32).astype(BF16), (rows == place + 4).astype(F32).astype(BF16)], axis=1)
    loads[4].wait()
    upper = jnp.concatenate(split(child[:, 0, :]), axis=1)
    lower = jnp.concatenate(split(child[:, 1, :]), axis=1)
    total = dot(hot, jnp.concatenate([upper, lower], axis=0))
    summed[...] = (total[:, :128] + total[:, 128:]).reshape(64, 8, 128)

    loads[5].wait()
    chosen = lax.broadcasted_iota(jnp.int32, (8, 128), 0) == col
    for b in range(4):
        order[b] = right[:, b * 128:b * 128 + 128]
        for kk in range(2):
            lines = jnp.where(chosen, order[b, pl.ds(kk, 8, stride=2), :], 0.0)
            rown[kk * 4 + b:kk * 4 + b + 1, :] = jnp.sum(lines, axis=0, keepdims=True)
    pown[0] = summed[first] + rown[...] * is_first
    pown[1] = summed[second] + rown[...] * is_second

    loads[6].wait()
    ig = z // 4
    dmine[...] = diag[0, pl.ds(pl.multiple_of(ig * 16, 16), 16), :].astype(F32)
    dfull[col] = diag[1].astype(F32)
    loads[7].wait()
    ffull[col] = fac[1].astype(F32)

    pl.semaphore_wait(barrier, len(peers))

    for s, d in enumerate(NEAR):
        put(0, pown.at[0], pz.at[0, s], z_peer(d))
    put(2, fmask.at[pl.ds(5, 4)], frelay.at[pl.ds(0, 4)], z_peer(4))
    put(2, fmask.at[pl.ds(9, 3)], frelay.at[pl.ds(4, 3)], z_peer(-4))
    for s, d in enumerate(NEAR):
        put(1, pown.at[1], pz.at[1, s], z_peer(d))
    for d in C_OFFS:
        put(3, dmine, dg.at[col], c_peer(d))
    dg[col] = dmine[...]
    for s, d in enumerate(X_OFFS):
        put(4, summed.at[pl.ds((x + d) % NX * NZ, NZ)], mx.at[s], x_peer(d))
    for group, full in ((11, dfull), (12, ffull)):
        for d in (2, 1, 3):
            put(group, full.at[col], full.at[col], c_peer((d, 0)))

    def panel_near(p):
        whole(p, pz.at[p]).wait_recv()
        above = pz[p, 1] + pz[p, 3] + pz[p, 5] + pz[p, 7]
        below = pz[p, 2] + pz[p, 4] + pz[p, 6]
        pside[p, 0] = below
        pside[p, 1] = above
        put(15 + p, pside.at[p, 0], pfar.at[p, 0], z_peer(4))
        put(15 + p, pside.at[p, 1], pfar.at[p, 1], z_peer(-4))
        pmine[p] = pown[p] + above + below + pz[p, 0]

    def panel_sum(p):
        whole(15 + p, pfar.at[p]).wait_recv()
        pmine[p] = pmine[p] + pfar[p, 0] + pfar[p, 1]
        for d in XC_OFFS:
            put(5 + p, pmine.at[p], px.at[p, (4 - d[0]) % 4 * 8 + col], xc_peer(d))
        px[p, col] = pmine[p]

    panel_near(0)
    whole(2, frelay).wait_recv()
    for s, d in enumerate(NEAR):
        if d == -4:
            fpass[s] = fmask[12]
        else:
            fpass[s] = fmask[d % NZ] + frelay[d - 1 if d > 0 else 7 + d]
        put(17, fpass.at[s], fz.at[s], z_peer(d))
    panel_near(1)

    panel_sum(0)
    whole(17, fz).wait_recv()
    fmine[...] = fmask[0] + jnp.sum(fz[...], axis=0)
    for d in XC_OFFS:
        put(7, fmine, fx.at[(4 - d[0]) % 4 * 8 + col], xc_peer(d))
    fx[col] = fmine[...]
    panel_sum(1)
    whole(4, mx).wait_recv()
    mmine[...] = summed[pl.ds(x * NZ, NZ)] + mx[0] + mx[1] + mx[2]
    for s, d in enumerate(Z_OFFS):
        put(8, mmine.at[(z + d) % NZ], mz.at[s], z_peer(d))

    def panel_state(p):
        whole(5 + p, px.at[p, pl.ds(0, 31)]).wait_recv()
        value = px[p, 0:8] + px[p, 8:16] + px[p, 16:24] + px[p, 24:32]
        xs[p] = value.reshape(64, 128)
        return jnp.concatenate(
            [jnp.concatenate([xs[p, pl.ds(kk * 4 + b, 8, stride=8), :] for kk in range(2)], axis=0) for b in range(4)],
            axis=1,
        )

    eye = (
        lax.broadcasted_iota(jnp.int32, (64, 512), 1) == lax.broadcasted_iota(jnp.int32, (64, 512), 0) + col * 64
    ).astype(F32)
    w_first = (eye * is_first - fac[0].astype(F32) * other).astype(BF16)

    state = stacked(panel_state(0))
    whole(3, dg.at[pl.ds(0, 7)]).wait_recv()
    group = folded(dot_t(state, dg[...].reshape(128, 512).astype(BF16)))
    whole(7, fx.at[pl.ds(0, 31)]).wait_recv()
    piece = (fx[0:8] + fx[8:16] + fx[16:24] + fx[24:32]).reshape(128, 128).astype(BF16)
    tz[z] = folded(dot(stacked(group), piece))
    for d in Z_OFFS:
        put(9, tz.at[z], tz.at[z], z_peer(d))

    solved = folded(dot_t(state, diag[0]))
    partial = folded(dot(stacked(solved), w_first))
    whole(8, mz).wait_recv()
    assembled = (mmine[z] + jnp.sum(mz[...], axis=0)) * other
    mine = lax.broadcasted_iota(jnp.int32, (8, 128), 0) == col
    placed = jnp.concatenate(
        [
            jnp.concatenate(
                [jnp.where(mine, assembled[kk * 4 + b:kk * 4 + b + 1, :], 0.0) for kk in range(2)], axis=0
            )
            for b in range(4)
        ],
        axis=1,
    )
    part[...] = partial + placed
    for s, d in enumerate(C_OFFS):
        put(10, part, pr.at[s], c_peer(d))
    for group, full in ((11, dfull), (12, ffull)):
        whole(group, full.at[pl.ds(0, 3)]).wait_recv()
        for d in range(4):
            index = (y + d) % NY * NC + k
            put(group + 2, full.at[index], full.at[index], c_peer((0, 1)))
    state = panel_state(1)
    whole(13, dfull.at[pl.ds(0, 4)]).wait_recv()
    dhalf[...] = dfull[...].reshape(512, 512).astype(BF16)
    whole(14, ffull.at[pl.ds(0, 4)]).wait_recv()
    fhalf[...] = ffull[...].reshape(512, 512).astype(BF16)
    whole(10, pr).wait_recv()
    total = part[...] + jnp.sum(pr[...], axis=0)

    whole(9, tz.at[pl.ds(0, 15)]).wait_recv()
    update = jnp.concatenate([tz[b] + tz[4 + b] + tz[8 + b] + tz[12 + b] for b in range(4)], axis=1)
    solved = folded(dot_t(stacked(state - update), dhalf[...]))
    total = total + solved * is_second - folded(dot(stacked(solved), fhalf[...])) * other
    for b in range(4):
        for kk in range(2):
            order[b, pl.ds(kk, 8, stride=2), :] = total[kk * 8:kk * 8 + 8, b * 128:b * 128 + 128]
        lanes = slice(b * 128, b * 128 + 128)
        out[:, lanes] = order[b] + right[:, lanes] * other

    whole(0, pz.at[0]).wait_send()
    whole(1, pz.at[1]).wait_send()
    whole(2, frelay).wait_send()
    whole(15, pfar.at[0]).wait_send()
    whole(16, pfar.at[1]).wait_send()
    whole(17, fz).wait_send()
    whole(3, dg.at[pl.ds(0, 7)]).wait_send()
    whole(4, mx).wait_send()
    whole(5, px.at[0, pl.ds(0, 31)]).wait_send()
    whole(6, px.at[1, pl.ds(0, 31)]).wait_send()
    whole(7, fx.at[pl.ds(0, 31)]).wait_send()
    whole(8, mz).wait_send()
    whole(9, tz.at[pl.ds(0, 15)]).wait_send()
    whole(10, pr).wait_send()
    for group, full in ((11, dfull), (12, ffull)):
        whole(group, full.at[pl.ds(0, 3)]).wait_send()
        whole(group + 2, full.at[pl.ds(0, 4)]).wait_send()


def body(right_side, child_updates, child_device, child_block, owners, diag_inverse, panel_factor):
    return pl.pallas_call(
        kernel,
        out_shape=jax.ShapeDtypeStruct((16, 512), F32),
        in_specs=[pl.BlockSpec(memory_space=pltpu.HBM)] * 7,
        out_specs=pl.BlockSpec(memory_space=pltpu.VMEM),
        scratch_shapes=[
            pltpu.SMEM((2,), jnp.int32),
            pltpu.VMEM((16, 512), F32),
            pltpu.VMEM((256, 2, 128), F32),
            pltpu.VMEM((1, 256), jnp.int32),
            pltpu.VMEM((1, 256), jnp.int32),
            pltpu.VMEM((2, 64, 512), BF16),
            pltpu.VMEM((2, 64, 512), BF16),
            pltpu.SemaphoreType.DMA((8,)),
            pltpu.VMEM((64, 8, 128), F32),
            pltpu.VMEM((16, 16, 128), F32),
            pltpu.VMEM((8, 16, 128), F32),
            pltpu.VMEM((16, 128), F32),
            pltpu.VMEM((32, 16, 128), F32),
            pltpu.VMEM((2, 8, 128), F32),
            pltpu.VMEM((2, 8, 8, 128), F32),
            pltpu.VMEM((2, 8, 128), F32),
            pltpu.VMEM((2, 32, 8, 128), F32),
            pltpu.VMEM((16, 512), F32),
            pltpu.VMEM((8, 16, 512), F32),
            pltpu.VMEM((3, 16, 8, 128), F32),
            pltpu.VMEM((16, 8, 128), F32),
            pltpu.VMEM((15, 8, 128), F32),
            pltpu.VMEM((16, 16, 128), F32),
            pltpu.VMEM((16, 512), F32),
            pltpu.VMEM((7, 16, 512), F32),
            pltpu.VMEM((2, 64, 128), F32),
            pltpu.VMEM((8, 128), F32),
            pltpu.VMEM((4, 16, 128), F32),
            pltpu.VMEM((8, 64, 512), F32),
            pltpu.VMEM((8, 64, 512), F32),
            pltpu.VMEM((512, 512), BF16),
            pltpu.VMEM((512, 512), BF16),
            pltpu.VMEM((2, 2, 8, 128), F32),
            pltpu.VMEM((2, 2, 8, 128), F32),
            pltpu.VMEM((7, 16, 128), F32),
            pltpu.VMEM((8, 16, 128), F32),
            pltpu.SemaphoreType.DMA((18,)),
            pltpu.SemaphoreType.DMA((18,)),
        ],
        compiler_params=pltpu.CompilerParams(
            collective_id=0, has_side_effects=True, vmem_limit_bytes=60 * 1024 * 1024
        ),
    )(
        owners, right_side, child_updates, child_device.reshape(1, 256), child_block.reshape(1, 256),
        diag_inverse, panel_factor,
    )


def solution(mesh):
    return jax.shard_map(
        body,
        mesh=mesh,
        in_specs=(
            P(None, "rows"),
            P("rows", "cols", None),
            P("rows", None),
            P("rows", None),
            P(),
            P(None, "cols", None),
            P(None, "cols", "rows"),
        ),
        out_specs=P(None, "rows"),
        check_vma=False,
    )
```

```python
import functools

import jax
import jax.numpy as jnp
from jax import lax
from jax.experimental import pallas as pl
from jax.experimental.pallas import tpu as pltpu
from jax.sharding import PartitionSpec as P

MESH = pl.DeviceIdType.MESH
F32, BF16 = jnp.float32, jnp.bfloat16
NX, NY, NC, NZ = 4, 4, 2, 16

EARLY, MIDDLE, LATE = (0, 1, 2), (3,), ()

NEAR = (4, -4, 3, -3, 2, -2, 1, -1)
RELAY = (4, -3, 3, -2, 2, -1, 1)
Z_OFFS = (8, 7, 9, 6, 10, 5, 11, 4, 12, 3, 13, 2, 14, 1, 15)
X_OFFS = (2, 1, 3)
C_OFFS = tuple((dy, dk) for dy in (2, 1, 3, 0) for dk in (0, 1) if dy or dk)
XC_OFFS = tuple((dx, dy, dk) for dx in (2, 1, 3, 0) for dy in (2, 1, 3, 0) for dk in (0, 1) if dx or dy or dk)


def split(value):
    high = value.astype(BF16)
    return high, (value - high.astype(F32)).astype(BF16)


def stacked(value):
    return jnp.concatenate(split(value), axis=0)


def folded(value):
    half = value.shape[0] // 2
    return value[:half] + value[half:]


def dot(a, b):
    return jnp.dot(a, b, preferred_element_type=F32)


def dot_t(a, b):
    return lax.dot_general(a, b, (((1,), (1,)), ((), ())), preferred_element_type=F32)


def kernel(
    owners_any, right_any, child_any, dev_any, blk_any, diag_any, fac_any, out,
    owners, right, child, dev, blk, diag, fac, local,
    summed, fmask, fz, fmine, fx, pown, pz, pmine, px, dg, mx, mmine, mz, tz, part, pr, xs, rown, order, dfull, ffull, dhalf, fhalf, pside, pfar, frelay, fpass, send, recv,
):
    row, col = lax.axis_index("rows"), lax.axis_index("cols")
    x, z, y, k = row // NZ, row % NZ, col // NC, col % NC

    def z_peer(d):
        return (x * NZ + (z + d + NZ) % NZ, col)

    def x_peer(d):
        return ((x + d) % NX * NZ + z, col)

    def c_peer(d):
        return (row, (y + d[0]) % NY * NC + (k + d[1]) % NC)

    def xc_peer(d):
        return ((x + d[0]) % NX * NZ + z, (y + d[1]) % NY * NC + (k + d[2]) % NC)

    loads = [
        pltpu.make_async_copy(src, dst, local.at[i])
        for i, (src, dst) in enumerate(
            [
                (owners_any, owners), (fac_any.at[0], fac.at[0]), (dev_any, dev), (blk_any, blk), (child_any, child),
                (right_any, right), (diag_any, diag), (fac_any.at[1], fac.at[1]),
            ]
        )
    ]
    for load in loads:
        load.start()

    barrier = pltpu.get_barrier_semaphore()
    peers = [z_peer(d) for d in NEAR] + [xc_peer(d) for d in XC_OFFS]
    for peer in peers:
        pl.semaphore_signal(barrier, inc=1, device_id=peer, device_id_type=MESH)

    def put(group, src, dst, peer):
        pltpu.make_async_remote_copy(src, dst, send.at[group], recv.at[group], device_id=peer, device_id_type=MESH).start()

    def relay_group(e):
        return 19 + RELAY.index(e)

    def whole(group, ref):
        return pltpu.make_async_remote_copy(
            ref, ref, send.at[group], recv.at[group], device_id=x_peer(1), device_id_type=MESH
        )

    loads[0].wait()
    first, second = owners[0], owners[1]
    is_first = (row == first).astype(F32)
    is_second = (row == second).astype(F32)
    other = (1.0 - is_first) * (1.0 - is_second)

    loads[1].wait()
    block = fac[0].astype(F32) * is_second
    for ig in range(4):
        for jb in range(4):
            fmask[(ig * 4 + jb - z + NZ) % NZ] = block[ig * 16:ig * 16 + 16, jb * 128:jb * 128 + 128]
    loads[2].wait()
    loads[3].wait()
    place = dev[...] * 8 + blk[...]
    rows = lax.broadcasted_iota(jnp.int32, (512, 256), 0)
    hot = jnp.concatenate([(rows == place).astype(F32).astype(BF16), (rows == place + 4).astype(F32).astype(BF16)], axis=1)
    loads[4].wait()
    upper = jnp.concatenate(split(child[:, 0, :]), axis=1)
    lower = jnp.concatenate(split(child[:, 1, :]), axis=1)
    total = dot(hot, jnp.concatenate([upper, lower], axis=0))
    summed[...] = (total[:, :128] + total[:, 128:]).reshape(64, 8, 128)

    loads[5].wait()
    chosen = lax.broadcasted_iota(jnp.int32, (8, 128), 0) == col
    for b in range(4):
        order[b] = right[:, b * 128:b * 128 + 128]
        for kk in range(2):
            lines = jnp.where(chosen, order[b, pl.ds(kk, 8, stride=2), :], 0.0)
            rown[kk * 4 + b:kk * 4 + b + 1, :] = jnp.sum(lines, axis=0, keepdims=True)
    pown[0] = summed[first] + rown[...] * is_first
    pown[1] = summed[second] + rown[...] * is_second

    loads[6].wait()
    ig = z // 4
    dg[col] = diag[0, pl.ds(pl.multiple_of(ig * 16, 16), 16), :].astype(F32)
    dfull[col] = diag[1].astype(F32)
    loads[7].wait()
    ffull[col] = fac[1].astype(F32)

    pl.semaphore_wait(barrier, len(peers))

    for s, d in enumerate(NEAR):
        put(0, pown.at[0], pz.at[0, s], z_peer(d))
    for e in RELAY:
        far = 4 if e > 0 else -4
        put(relay_group(e), fmask.at[(e + far) % NZ], frelay.at[e % 8], z_peer(far))
    put(17, fmask.at[12], fz.at[7], z_peer(-4))
    for d in (2, 1, 3):
        put(3, dg.at[col], dg.at[col], c_peer((d, 0)))
    for s, d in enumerate(X_OFFS):
        put(4, summed.at[pl.ds((x + d) % NX * NZ, NZ)], mx.at[s], x_peer(d))
    def half(part, index):
        return (dfull if part < 2 else ffull).at[index, pl.ds(part % 2 * 32, 32)]

    def halves(part):
        return (dfull if part < 2 else ffull).at[pl.ds(0, 4), pl.ds(0, 32)]

    def three(part):
        return (dfull if part < 2 else ffull).at[pl.ds(0, 3), pl.ds(0, 32)]

    def gather(parts):
        for part in parts:
            for d in (2, 1, 3):
                put(26 + part, half(part, col), half(part, col), c_peer((d, 0)))

    def forward(parts):
        for part in parts:
            whole(26 + part, three(part)).wait_recv()
            for d in range(4):
                index = (y + d) % NY * NC + k
                put(30 + part, half(part, index), half(part, index), c_peer((0, 1)))

    gather(EARLY)

    def panel_near(p):
        whole(p, pz.at[p]).wait_recv()
        above = pz[p, 1] + pz[p, 3] + pz[p, 5] + pz[p, 7]
        below = pz[p, 2] + pz[p, 4] + pz[p, 6]
        pside[p, 0] = below
        pside[p, 1] = above
        put(15 + p, pside.at[p, 0], pfar.at[p, 0], z_peer(4))
        put(15 + p, pside.at[p, 1], pfar.at[p, 1], z_peer(-4))
        pmine[p] = pown[p] + above + below + pz[p, 0]

    def panel_sum(p):
        whole(15 + p, pfar.at[p]).wait_recv()
        pmine[p] = pmine[p] + pfar[p, 0] + pfar[p, 1]
        for d in XC_OFFS:
            put(5 + p, pmine.at[p], px.at[p, (4 - d[0]) % 4 * 8 + col], xc_peer(d))
        px[p, col] = pmine[p]

    panel_near(0)
    for s, e in enumerate(RELAY):
        whole(relay_group(e), frelay.at[e % 8]).wait_recv()
        fpass[s] = fmask[e % NZ] + frelay[e % 8]
        put(17, fpass.at[s], fz.at[s], z_peer(e))
    for s, d in enumerate(NEAR):
        put(1, pown.at[1], pz.at[1, s], z_peer(d))

    whole(3, dg.at[pl.ds(0, 3)]).wait_recv()
    for d in range(4):
        index = (y + d) % NY * NC + k
        put(18, dg.at[index], dg.at[index], c_peer((0, 1)))
    panel_sum(0)
    whole(17, fz).wait_recv()
    fmine[...] = fmask[0] + jnp.sum(fz[...], axis=0)
    for d in XC_OFFS:
        put(7, fmine, fx.at[(4 - d[0]) % 4 * 8 + col], xc_peer(d))
    fx[col] = fmine[...]
    panel_near(1)
    whole(4, mx).wait_recv()
    mmine[...] = summed[pl.ds(x * NZ, NZ)] + mx[0] + mx[1] + mx[2]
    for s, d in enumerate(Z_OFFS):
        put(8, mmine.at[(z + d) % NZ], mz.at[s], z_peer(d))

    def panel_state(p):
        whole(5 + p, px.at[p, pl.ds(0, 31)]).wait_recv()
        value = px[p, 0:8] + px[p, 8:16] + px[p, 16:24] + px[p, 24:32]
        xs[p] = value.reshape(64, 128)
        return jnp.concatenate(
            [jnp.concatenate([xs[p, pl.ds(kk * 4 + b, 8, stride=8), :] for kk in range(2)], axis=0) for b in range(4)],
            axis=1,
        )

    eye = (
        lax.broadcasted_iota(jnp.int32, (64, 512), 1) == lax.broadcasted_iota(jnp.int32, (64, 512), 0) + col * 64
    ).astype(F32)
    w_first = (eye * is_first - fac[0].astype(F32) * other).astype(BF16)

    state = stacked(panel_state(0))
    whole(18, dg.at[pl.ds(0, 4)]).wait_recv()
    group = folded(dot_t(state, dg[...].reshape(128, 512).astype(BF16)))
    panel_sum(1)
    gather(MIDDLE)
    whole(7, fx.at[pl.ds(0, 31)]).wait_recv()
    piece = (fx[0:8] + fx[8:16] + fx[16:24] + fx[24:32]).reshape(128, 128).astype(BF16)
    tz[z] = folded(dot(stacked(group), piece))
    for d in Z_OFFS:
        put(9, tz.at[z], tz.at[z], z_peer(d))
    gather(LATE)

    solved = folded(dot_t(state, diag[0]))
    partial = folded(dot(stacked(solved), w_first))
    whole(8, mz).wait_recv()
    assembled = (mmine[z] + jnp.sum(mz[...], axis=0)) * other
    mine = lax.broadcasted_iota(jnp.int32, (8, 128), 0) == col
    placed = jnp.concatenate(
        [
            jnp.concatenate(
                [jnp.where(mine, assembled[kk * 4 + b:kk * 4 + b + 1, :], 0.0) for kk in range(2)], axis=0
            )
            for b in range(4)
        ],
        axis=1,
    )
    part[...] = partial + placed
    for s, d in enumerate(C_OFFS):
        put(10, part, pr.at[s], c_peer(d))
    forward(EARLY)
    state = panel_state(1)
    forward(MIDDLE)
    whole(10, pr).wait_recv()
    total = part[...] + jnp.sum(pr[...], axis=0)
    forward(LATE)
    for part_ in range(4):
        whole(30 + part_, halves(part_)).wait_recv()
    dhalf[...] = dfull[...].reshape(512, 512).astype(BF16)
    fhalf[...] = ffull[...].reshape(512, 512).astype(BF16)

    whole(9, tz.at[pl.ds(0, 15)]).wait_recv()
    update = jnp.concatenate([tz[b] + tz[4 + b] + tz[8 + b] + tz[12 + b] for b in range(4)], axis=1)
    solved = folded(dot_t(stacked(state - update), dhalf[...]))
    total = total + solved * is_second - folded(dot(stacked(solved), fhalf[...])) * other
    for b in range(4):
        for kk in range(2):
            order[b, pl.ds(kk, 8, stride=2), :] = total[kk * 8:kk * 8 + 8, b * 128:b * 128 + 128]
        lanes = slice(b * 128, b * 128 + 128)
        out[:, lanes] = order[b] + right[:, lanes] * other

    whole(0, pz.at[0]).wait_send()
    whole(1, pz.at[1]).wait_send()
    for e in RELAY:
        whole(relay_group(e), frelay.at[e % 8]).wait_send()
    whole(15, pfar.at[0]).wait_send()
    whole(16, pfar.at[1]).wait_send()
    whole(17, fz).wait_send()
    whole(3, dg.at[pl.ds(0, 3)]).wait_send()
    whole(18, dg.at[pl.ds(0, 4)]).wait_send()
    whole(4, mx).wait_send()
    whole(5, px.at[0, pl.ds(0, 31)]).wait_send()
    whole(6, px.at[1, pl.ds(0, 31)]).wait_send()
    whole(7, fx.at[pl.ds(0, 31)]).wait_send()
    whole(8, mz).wait_send()
    whole(9, tz.at[pl.ds(0, 15)]).wait_send()
    whole(10, pr).wait_send()
    for part_ in range(4):
        whole(26 + part_, three(part_)).wait_send()
        whole(30 + part_, halves(part_)).wait_send()


def body(right_side, child_updates, child_device, child_block, owners, diag_inverse, panel_factor):
    return pl.pallas_call(
        kernel,
        out_shape=jax.ShapeDtypeStruct((16, 512), F32),
        in_specs=[pl.BlockSpec(memory_space=pltpu.HBM)] * 7,
        out_specs=pl.BlockSpec(memory_space=pltpu.VMEM),
        scratch_shapes=[
            pltpu.SMEM((2,), jnp.int32),
            pltpu.VMEM((16, 512), F32),
            pltpu.VMEM((256, 2, 128), F32),
            pltpu.VMEM((1, 256), jnp.int32),
            pltpu.VMEM((1, 256), jnp.int32),
            pltpu.VMEM((2, 64, 512), BF16),
            pltpu.VMEM((2, 64, 512), BF16),
            pltpu.SemaphoreType.DMA((8,)),
            pltpu.VMEM((64, 8, 128), F32),
            pltpu.VMEM((16, 16, 128), F32),
            pltpu.VMEM((8, 16, 128), F32),
            pltpu.VMEM((16, 128), F32),
            pltpu.VMEM((32, 16, 128), F32),
            pltpu.VMEM((2, 8, 128), F32),
            pltpu.VMEM((2, 8, 8, 128), F32),
            pltpu.VMEM((2, 8, 128), F32),
            pltpu.VMEM((2, 32, 8, 128), F32),
            pltpu.VMEM((8, 16, 512), F32),
            pltpu.VMEM((3, 16, 8, 128), F32),
            pltpu.VMEM((16, 8, 128), F32),
            pltpu.VMEM((15, 8, 128), F32),
            pltpu.VMEM((16, 16, 128), F32),
            pltpu.VMEM((16, 512), F32),
            pltpu.VMEM((7, 16, 512), F32),
            pltpu.VMEM((2, 64, 128), F32),
            pltpu.VMEM((8, 128), F32),
            pltpu.VMEM((4, 16, 128), F32),
            pltpu.VMEM((8, 64, 512), F32),
            pltpu.VMEM((8, 64, 512), F32),
            pltpu.VMEM((512, 512), BF16),
            pltpu.VMEM((512, 512), BF16),
            pltpu.VMEM((2, 2, 8, 128), F32),
            pltpu.VMEM((2, 2, 8, 128), F32),
            pltpu.VMEM((8, 16, 128), F32),
            pltpu.VMEM((7, 16, 128), F32),
            pltpu.SemaphoreType.DMA((34,)),
            pltpu.SemaphoreType.DMA((34,)),
        ],
        compiler_params=pltpu.CompilerParams(
            collective_id=0, has_side_effects=True, vmem_limit_bytes=60 * 1024 * 1024
        ),
    )(
        owners, right_side, child_updates, child_device.reshape(1, 256), child_block.reshape(1, 256),
        diag_inverse, panel_factor,
    )


def solution(mesh):
    return jax.shard_map(
        body,
        mesh=mesh,
        in_specs=(
            P(None, "rows"),
            P("rows", "cols", None),
            P("rows", None),
            P("rows", None),
            P(),
            P(None, "cols", None),
            P(None, "cols", "rows"),
        ),
        out_specs=P(None, "rows"),
        check_vma=False,
    )
```

```python
import functools

import jax
import jax.numpy as jnp
from jax import lax
from jax.experimental import pallas as pl
from jax.experimental.pallas import tpu as pltpu
from jax.sharding import PartitionSpec as P

MESH = pl.DeviceIdType.MESH
F32, BF16 = jnp.float32, jnp.bfloat16
NX, NY, NC, NZ = 4, 4, 2, 16

EARLY, MIDDLE, LATE = (0, 1, 2), (3,), ()

NEAR = (4, -4, 3, -3, 2, -2, 1, -1)
RELAY = (4, -3, 3, -2, 2, -1, 1)
Z_OFFS = (8, 7, 9, 6, 10, 5, 11, 4, 12, 3, 13, 2, 14, 1, 15)
X_OFFS = (2, 1, 3)
C_OFFS = tuple((dy, dk) for dy in (2, 1, 3, 0) for dk in (0, 1) if dy or dk)
XC_OFFS = tuple((dx, dy, dk) for dx in (2, 1, 3, 0) for dy in (2, 1, 3, 0) for dk in (0, 1) if dx or dy or dk)


def split(value):
    high = value.astype(BF16)
    return high, (value - high.astype(F32)).astype(BF16)


def stacked(value):
    return jnp.concatenate(split(value), axis=0)


def folded(value):
    half = value.shape[0] // 2
    return value[:half] + value[half:]


def dot(a, b):
    return jnp.dot(a, b, preferred_element_type=F32)


def dot_t(a, b):
    return lax.dot_general(a, b, (((1,), (1,)), ((), ())), preferred_element_type=F32)


def kernel(
    owners_any, right_any, child_any, dev_any, blk_any, diag_any, fac_any, out,
    owners, right, child, dev, blk, diag, fac, local,
    summed, fmask, fz, fmine, fx, pown, pz, pmine, px, dg, mx, mmine, mz, tz, part, pr, pair, xs, rown, order, dfull, ffull, dhalf, fhalf, pside, pfar, frelay, fpass, send, recv,
):
    row, col = lax.axis_index("rows"), lax.axis_index("cols")
    x, z, y, k = row // NZ, row % NZ, col // NC, col % NC

    def z_peer(d):
        return (x * NZ + (z + d + NZ) % NZ, col)

    def x_peer(d):
        return ((x + d) % NX * NZ + z, col)

    def c_peer(d):
        return (row, (y + d[0]) % NY * NC + (k + d[1]) % NC)

    def xc_peer(d):
        return ((x + d[0]) % NX * NZ + z, (y + d[1]) % NY * NC + (k + d[2]) % NC)

    loads = [
        pltpu.make_async_copy(src, dst, local.at[i])
        for i, (src, dst) in enumerate(
            [
                (owners_any, owners), (fac_any.at[0], fac.at[0]), (dev_any, dev), (blk_any, blk), (child_any, child),
                (right_any, right), (diag_any, diag), (fac_any.at[1], fac.at[1]),
            ]
        )
    ]
    for load in loads:
        load.start()

    barrier = pltpu.get_barrier_semaphore()
    peers = [z_peer(d) for d in NEAR] + [xc_peer(d) for d in XC_OFFS]
    for peer in peers:
        pl.semaphore_signal(barrier, inc=1, device_id=peer, device_id_type=MESH)

    def put(group, src, dst, peer):
        pltpu.make_async_remote_copy(src, dst, send.at[group], recv.at[group], device_id=peer, device_id_type=MESH).start()

    def relay_group(e):
        return 19 + RELAY.index(e)

    def whole(group, ref):
        return pltpu.make_async_remote_copy(
            ref, ref, send.at[group], recv.at[group], device_id=x_peer(1), device_id_type=MESH
        )

    loads[0].wait()
    first, second = owners[0], owners[1]
    is_first = (row == first).astype(F32)
    is_second = (row == second).astype(F32)
    other = (1.0 - is_first) * (1.0 - is_second)

    loads[1].wait()
    block = fac[0].astype(F32) * is_second
    for ig in range(4):
        for jb in range(4):
            fmask[(ig * 4 + jb - z + NZ) % NZ] = block[ig * 16:ig * 16 + 16, jb * 128:jb * 128 + 128]
    loads[2].wait()
    loads[3].wait()
    place = dev[...] * 8 + blk[...]
    rows = lax.broadcasted_iota(jnp.int32, (512, 256), 0)
    hot = jnp.concatenate([(rows == place).astype(F32).astype(BF16), (rows == place + 4).astype(F32).astype(BF16)], axis=1)
    loads[4].wait()
    upper = jnp.concatenate(split(child[:, 0, :]), axis=1)
    lower = jnp.concatenate(split(child[:, 1, :]), axis=1)
    total = dot(hot, jnp.concatenate([upper, lower], axis=0))
    summed[...] = (total[:, :128] + total[:, 128:]).reshape(64, 8, 128)

    loads[5].wait()
    chosen = lax.broadcasted_iota(jnp.int32, (8, 128), 0) == col
    for b in range(4):
        order[b] = right[:, b * 128:b * 128 + 128]
        for kk in range(2):
            lines = jnp.where(chosen, order[b, pl.ds(kk, 8, stride=2), :], 0.0)
            rown[kk * 4 + b:kk * 4 + b + 1, :] = jnp.sum(lines, axis=0, keepdims=True)
    pown[0] = summed[first] + rown[...] * is_first
    pown[1] = summed[second] + rown[...] * is_second

    loads[6].wait()
    ig = z // 4
    dg[col] = diag[0, pl.ds(pl.multiple_of(ig * 16, 16), 16), :].astype(F32)
    dfull[col] = diag[1].astype(F32)
    loads[7].wait()
    ffull[col] = fac[1].astype(F32)

    pl.semaphore_wait(barrier, len(peers))

    for s, d in enumerate(NEAR):
        put(0, pown.at[0], pz.at[0, s], z_peer(d))
    for e in RELAY:
        far = 4 if e > 0 else -4
        put(relay_group(e), fmask.at[(e + far) % NZ], frelay.at[e % 8], z_peer(far))
    put(17, fmask.at[12], fz.at[7], z_peer(-4))
    for d in (2, 1, 3):
        put(3, dg.at[col], dg.at[col], c_peer((d, 0)))
    for s, d in enumerate(X_OFFS):
        put(4, summed.at[pl.ds((x + d) % NX * NZ, NZ)], mx.at[s], x_peer(d))
    def half(part, index):
        return (dfull if part < 2 else ffull).at[index, pl.ds(part % 2 * 32, 32)]

    def halves(part):
        return (dfull if part < 2 else ffull).at[pl.ds(0, 4), pl.ds(0, 32)]

    def three(part):
        return (dfull if part < 2 else ffull).at[pl.ds(0, 3), pl.ds(0, 32)]

    def gather(parts):
        for part in parts:
            for d in (2, 1, 3):
                put(26 + part, half(part, col), half(part, col), c_peer((d, 0)))

    def forward(parts):
        for part in parts:
            whole(26 + part, three(part)).wait_recv()
            for d in range(4):
                index = (y + d) % NY * NC + k
                put(30 + part, half(part, index), half(part, index), c_peer((0, 1)))

    gather(EARLY)

    def panel_near(p):
        whole(p, pz.at[p]).wait_recv()
        above = pz[p, 1] + pz[p, 3] + pz[p, 5] + pz[p, 7]
        below = pz[p, 2] + pz[p, 4] + pz[p, 6]
        pside[p, 0] = below
        pside[p, 1] = above
        put(15 + p, pside.at[p, 0], pfar.at[p, 0], z_peer(4))
        put(15 + p, pside.at[p, 1], pfar.at[p, 1], z_peer(-4))
        pmine[p] = pown[p] + above + below + pz[p, 0]

    def panel_sum(p):
        whole(15 + p, pfar.at[p]).wait_recv()
        pmine[p] = pmine[p] + pfar[p, 0] + pfar[p, 1]
        for d in XC_OFFS:
            put(5 + p, pmine.at[p], px.at[p, (4 - d[0]) % 4 * 8 + col], xc_peer(d))
        px[p, col] = pmine[p]

    panel_near(0)
    for s, e in enumerate(RELAY):
        whole(relay_group(e), frelay.at[e % 8]).wait_recv()
        fpass[s] = fmask[e % NZ] + frelay[e % 8]
        put(17, fpass.at[s], fz.at[s], z_peer(e))
    for s, d in enumerate(NEAR):
        put(1, pown.at[1], pz.at[1, s], z_peer(d))

    whole(3, dg.at[pl.ds(0, 3)]).wait_recv()
    for d in range(4):
        index = (y + d) % NY * NC + k
        put(18, dg.at[index], dg.at[index], c_peer((0, 1)))
    panel_sum(0)
    whole(17, fz).wait_recv()
    fmine[...] = fmask[0] + jnp.sum(fz[...], axis=0)
    for d in XC_OFFS:
        put(7, fmine, fx.at[(4 - d[0]) % 4 * 8 + col], xc_peer(d))
    fx[col] = fmine[...]
    panel_near(1)
    whole(4, mx).wait_recv()
    mmine[...] = summed[pl.ds(x * NZ, NZ)] + mx[0] + mx[1] + mx[2]
    for s, d in enumerate(Z_OFFS):
        put(8, mmine.at[(z + d) % NZ], mz.at[s], z_peer(d))

    def panel_state(p):
        whole(5 + p, px.at[p, pl.ds(0, 31)]).wait_recv()
        value = px[p, 0:8] + px[p, 8:16] + px[p, 16:24] + px[p, 24:32]
        xs[p] = value.reshape(64, 128)
        return jnp.concatenate(
            [jnp.concatenate([xs[p, pl.ds(kk * 4 + b, 8, stride=8), :] for kk in range(2)], axis=0) for b in range(4)],
            axis=1,
        )

    eye = (
        lax.broadcasted_iota(jnp.int32, (64, 512), 1) == lax.broadcasted_iota(jnp.int32, (64, 512), 0) + col * 64
    ).astype(F32)
    w_first = (eye * is_first - fac[0].astype(F32) * other).astype(BF16)

    state = stacked(panel_state(0))
    whole(18, dg.at[pl.ds(0, 4)]).wait_recv()
    group = folded(dot_t(state, dg[...].reshape(128, 512).astype(BF16)))
    panel_sum(1)
    gather(MIDDLE)
    whole(7, fx.at[pl.ds(0, 31)]).wait_recv()
    piece = (fx[0:8] + fx[8:16] + fx[16:24] + fx[24:32]).reshape(128, 128).astype(BF16)
    tz[z] = folded(dot(stacked(group), piece))
    for d in Z_OFFS:
        put(9, tz.at[z], tz.at[z], z_peer(d))
    gather(LATE)

    solved = folded(dot_t(state, diag[0]))
    partial = folded(dot(stacked(solved), w_first))
    whole(8, mz).wait_recv()
    assembled = (mmine[z] + jnp.sum(mz[...], axis=0)) * other
    mine = lax.broadcasted_iota(jnp.int32, (8, 128), 0) == col
    placed = jnp.concatenate(
        [
            jnp.concatenate(
                [jnp.where(mine, assembled[kk * 4 + b:kk * 4 + b + 1, :], 0.0) for kk in range(2)], axis=0
            )
            for b in range(4)
        ],
        axis=1,
    )
    part[...] = partial + placed
    put(10, part, pair, c_peer((0, 1)))
    forward(EARLY)
    whole(10, pair).wait_recv()
    whole(10, pair).wait_send()
    part[...] = part[...] + pair[...]
    for s, d in enumerate((2, 1, 3)):
        put(11, part, pr.at[s], c_peer((d, 0)))
    state = panel_state(1)
    forward(MIDDLE)
    whole(11, pr).wait_recv()
    total = part[...] + jnp.sum(pr[...], axis=0)
    forward(LATE)
    for part_ in range(4):
        whole(30 + part_, halves(part_)).wait_recv()
    dhalf[...] = dfull[...].reshape(512, 512).T.astype(BF16)
    fhalf[...] = ffull[...].reshape(512, 512).astype(BF16)

    whole(9, tz.at[pl.ds(0, 15)]).wait_recv()
    update = jnp.concatenate([tz[b] + tz[4 + b] + tz[8 + b] + tz[12 + b] for b in range(4)], axis=1)
    solved = folded(dot(stacked(state - update), dhalf[...]))
    total = total + solved * is_second - folded(dot(stacked(solved), fhalf[...])) * other
    for b in range(4):
        for kk in range(2):
            order[b, pl.ds(kk, 8, stride=2), :] = total[kk * 8:kk * 8 + 8, b * 128:b * 128 + 128]
        lanes = slice(b * 128, b * 128 + 128)
        out[:, lanes] = order[b] + right[:, lanes] * other

    whole(0, pz.at[0]).wait_send()
    whole(1, pz.at[1]).wait_send()
    for e in RELAY:
        whole(relay_group(e), frelay.at[e % 8]).wait_send()
    whole(15, pfar.at[0]).wait_send()
    whole(16, pfar.at[1]).wait_send()
    whole(17, fz).wait_send()
    whole(3, dg.at[pl.ds(0, 3)]).wait_send()
    whole(18, dg.at[pl.ds(0, 4)]).wait_send()
    whole(4, mx).wait_send()
    whole(5, px.at[0, pl.ds(0, 31)]).wait_send()
    whole(6, px.at[1, pl.ds(0, 31)]).wait_send()
    whole(7, fx.at[pl.ds(0, 31)]).wait_send()
    whole(8, mz).wait_send()
    whole(9, tz.at[pl.ds(0, 15)]).wait_send()
    whole(11, pr).wait_send()
    for part_ in range(4):
        whole(26 + part_, three(part_)).wait_send()
        whole(30 + part_, halves(part_)).wait_send()


def body(right_side, child_updates, child_device, child_block, owners, diag_inverse, panel_factor):
    return pl.pallas_call(
        kernel,
        out_shape=jax.ShapeDtypeStruct((16, 512), F32),
        in_specs=[pl.BlockSpec(memory_space=pltpu.HBM)] * 7,
        out_specs=pl.BlockSpec(memory_space=pltpu.VMEM),
        scratch_shapes=[
            pltpu.SMEM((2,), jnp.int32),
            pltpu.VMEM((16, 512), F32),
            pltpu.VMEM((256, 2, 128), F32),
            pltpu.VMEM((1, 256), jnp.int32),
            pltpu.VMEM((1, 256), jnp.int32),
            pltpu.VMEM((2, 64, 512), BF16),
            pltpu.VMEM((2, 64, 512), BF16),
            pltpu.SemaphoreType.DMA((8,)),
            pltpu.VMEM((64, 8, 128), F32),
            pltpu.VMEM((16, 16, 128), F32),
            pltpu.VMEM((8, 16, 128), F32),
            pltpu.VMEM((16, 128), F32),
            pltpu.VMEM((32, 16, 128), F32),
            pltpu.VMEM((2, 8, 128), F32),
            pltpu.VMEM((2, 8, 8, 128), F32),
            pltpu.VMEM((2, 8, 128), F32),
            pltpu.VMEM((2, 32, 8, 128), F32),
            pltpu.VMEM((8, 16, 512), F32),
            pltpu.VMEM((3, 16, 8, 128), F32),
            pltpu.VMEM((16, 8, 128), F32),
            pltpu.VMEM((15, 8, 128), F32),
            pltpu.VMEM((16, 16, 128), F32),
            pltpu.VMEM((16, 512), F32),
            pltpu.VMEM((3, 16, 512), F32),
            pltpu.VMEM((16, 512), F32),
            pltpu.VMEM((2, 64, 128), F32),
            pltpu.VMEM((8, 128), F32),
            pltpu.VMEM((4, 16, 128), F32),
            pltpu.VMEM((8, 64, 512), F32),
            pltpu.VMEM((8, 64, 512), F32),
            pltpu.VMEM((512, 512), BF16),
            pltpu.VMEM((512, 512), BF16),
            pltpu.VMEM((2, 2, 8, 128), F32),
            pltpu.VMEM((2, 2, 8, 128), F32),
            pltpu.VMEM((8, 16, 128), F32),
            pltpu.VMEM((7, 16, 128), F32),
            pltpu.SemaphoreType.DMA((34,)),
            pltpu.SemaphoreType.DMA((34,)),
        ],
        compiler_params=pltpu.CompilerParams(
            collective_id=0, has_side_effects=True, vmem_limit_bytes=60 * 1024 * 1024
        ),
    )(
        owners, right_side, child_updates, child_device.reshape(1, 256), child_block.reshape(1, 256),
        diag_inverse, panel_factor,
    )


def solution(mesh):
    return jax.shard_map(
        body,
        mesh=mesh,
        in_specs=(
            P(None, "rows"),
            P("rows", "cols", None),
            P("rows", None),
            P("rows", None),
            P(),
            P(None, "cols", None),
            P(None, "cols", "rows"),
        ),
        out_specs=P(None, "rows"),
        check_vma=False,
    )
```

```python
import functools

import jax
import jax.numpy as jnp
from jax import lax
from jax.experimental import pallas as pl
from jax.experimental.pallas import tpu as pltpu
from jax.sharding import PartitionSpec as P

MESH = pl.DeviceIdType.MESH
F32, BF16 = jnp.float32, jnp.bfloat16
NX, NY, NC, NZ = 4, 4, 2, 16

EARLY, MIDDLE, LATE = (0, 1, 2), (3,), ()

NEAR = (4, -4, 3, -3, 2, -2, 1, -1)
RELAY = (4, -3, 3, -2, 2, -1, 1)
Z_OFFS = (8, 7, 9, 6, 10, 5, 11, 4, 12, 3, 13, 2, 14, 1, 15)
X_OFFS = (2, 1, 3)
C_OFFS = tuple((dy, dk) for dy in (2, 1, 3, 0) for dk in (0, 1) if dy or dk)
XC_OFFS = tuple((dx, dy, dk) for dx in (2, 1, 3, 0) for dy in (2, 1, 3, 0) for dk in (0, 1) if dx or dy or dk)


def split(value):
    high = value.astype(BF16)
    return high, (value - high.astype(F32)).astype(BF16)


def stacked(value):
    return jnp.concatenate(split(value), axis=0)


def folded(value):
    half = value.shape[0] // 2
    return value[:half] + value[half:]


def dot(a, b):
    return jnp.dot(a, b, preferred_element_type=F32)


def dot_t(a, b):
    return lax.dot_general(a, b, (((1,), (1,)), ((), ())), preferred_element_type=F32)


def kernel(
    owners_any, right_any, child_any, dev_any, blk_any, diag_any, fac_any, out,
    owners, right, child, dev, blk, diag, fac, local,
    summed, fmask, fz, fmine, fx, pown, pz, pmine, px, dg, mx, mmine, mz, tz, part, pr, pair, xs, rown, order, dfull, ffull, dhalf, fhalf, pside, pfar, frelay, fpass, send, recv,
):
    row, col = lax.axis_index("rows"), lax.axis_index("cols")
    x, z, y, k = row // NZ, row % NZ, col // NC, col % NC

    def z_peer(d):
        return (x * NZ + (z + d + NZ) % NZ, col)

    def x_peer(d):
        return ((x + d) % NX * NZ + z, col)

    def c_peer(d):
        return (row, (y + d[0]) % NY * NC + (k + d[1]) % NC)

    def xc_peer(d):
        return ((x + d[0]) % NX * NZ + z, (y + d[1]) % NY * NC + (k + d[2]) % NC)

    loads = [
        pltpu.make_async_copy(src, dst, local.at[i])
        for i, (src, dst) in enumerate(
            [
                (owners_any, owners), (fac_any.at[0], fac.at[0]), (dev_any, dev), (blk_any, blk), (child_any, child),
                (right_any, right), (diag_any, diag), (fac_any.at[1], fac.at[1]),
            ]
        )
    ]
    for load in loads:
        load.start()

    barrier = pltpu.get_barrier_semaphore()
    peers = [z_peer(d) for d in NEAR] + [xc_peer(d) for d in XC_OFFS]
    for peer in peers:
        pl.semaphore_signal(barrier, inc=1, device_id=peer, device_id_type=MESH)

    def put(group, src, dst, peer):
        pltpu.make_async_remote_copy(src, dst, send.at[group], recv.at[group], device_id=peer, device_id_type=MESH).start()

    def relay_group(e):
        return 19 + RELAY.index(e)

    def whole(group, ref):
        return pltpu.make_async_remote_copy(
            ref, ref, send.at[group], recv.at[group], device_id=x_peer(1), device_id_type=MESH
        )

    loads[0].wait()
    first, second = owners[0], owners[1]
    is_first = (row == first).astype(F32)
    is_second = (row == second).astype(F32)
    other = (1.0 - is_first) * (1.0 - is_second)

    loads[1].wait()
    block = fac[0].astype(F32) * is_second
    for ig in range(4):
        for jb in range(4):
            fmask[(ig * 4 + jb - z + NZ) % NZ] = block[ig * 16:ig * 16 + 16, jb * 128:jb * 128 + 128]
    loads[2].wait()
    loads[3].wait()
    place = dev[...] * 8 + blk[...]
    rows = lax.broadcasted_iota(jnp.int32, (512, 256), 0)
    hot = jnp.concatenate([(rows == place).astype(F32).astype(BF16), (rows == place + 4).astype(F32).astype(BF16)], axis=1)
    loads[4].wait()
    upper = jnp.concatenate(split(child[:, 0, :]), axis=1)
    lower = jnp.concatenate(split(child[:, 1, :]), axis=1)
    total = dot(hot, jnp.concatenate([upper, lower], axis=0))
    summed[...] = (total[:, :128] + total[:, 128:]).reshape(64, 8, 128)

    loads[5].wait()
    chosen = lax.broadcasted_iota(jnp.int32, (8, 128), 0) == col
    for b in range(4):
        order[b] = right[:, b * 128:b * 128 + 128]
        for kk in range(2):
            lines = jnp.where(chosen, order[b, pl.ds(kk, 8, stride=2), :], 0.0)
            rown[kk * 4 + b:kk * 4 + b + 1, :] = jnp.sum(lines, axis=0, keepdims=True)
    pown[0] = summed[first] + rown[...] * is_first
    pown[1] = summed[second] + rown[...] * is_second

    loads[6].wait()
    ig = z // 4
    dg[col] = diag[0, pl.ds(pl.multiple_of(ig * 16, 16), 16), :].astype(F32)
    dfull[col] = diag[1].astype(F32)
    loads[7].wait()
    ffull[col] = fac[1].astype(F32)

    pl.semaphore_wait(barrier, len(peers))

    for s, d in enumerate(NEAR):
        put(0, pown.at[0], pz.at[0, s], z_peer(d))
    for e in RELAY:
        far = 4 if e > 0 else -4
        put(relay_group(e), fmask.at[(e + far) % NZ], frelay.at[e % 8], z_peer(far))
    put(17, fmask.at[12], fz.at[7], z_peer(-4))
    for s, d in enumerate(X_OFFS):
        put(4, summed.at[pl.ds((x + d) % NX * NZ, NZ)], mx.at[s], x_peer(d))
    def half(part, index):
        return (dfull if part < 2 else ffull).at[index, pl.ds(part % 2 * 32, 32)]

    def halves(part):
        return (dfull if part < 2 else ffull).at[pl.ds(0, 4), pl.ds(0, 32)]

    def three(part):
        return (dfull if part < 2 else ffull).at[pl.ds(0, 3), pl.ds(0, 32)]

    def gather(parts):
        for part in parts:
            for d in (2, 1, 3):
                put(26 + part, half(part, col), half(part, col), c_peer((d, 0)))

    def forward(parts):
        for part in parts:
            whole(26 + part, three(part)).wait_recv()
            for d in range(4):
                index = (y + d) % NY * NC + k
                put(30 + part, half(part, index), half(part, index), c_peer((0, 1)))

    gather(EARLY[:1])
    for d in (2, 1, 3):
        put(3, dg.at[col], dg.at[col], c_peer((d, 0)))
    gather(EARLY[1:])

    def panel_near(p):
        whole(p, pz.at[p]).wait_recv()
        above = pz[p, 1] + pz[p, 3] + pz[p, 5] + pz[p, 7]
        below = pz[p, 2] + pz[p, 4] + pz[p, 6]
        pside[p, 0] = below
        pside[p, 1] = above
        put(15 + p, pside.at[p, 0], pfar.at[p, 0], z_peer(4))
        put(15 + p, pside.at[p, 1], pfar.at[p, 1], z_peer(-4))
        pmine[p] = pown[p] + above + below + pz[p, 0]

    def panel_sum(p):
        whole(15 + p, pfar.at[p]).wait_recv()
        pmine[p] = pmine[p] + pfar[p, 0] + pfar[p, 1]
        for d in XC_OFFS:
            put(5 + p, pmine.at[p], px.at[p, (4 - d[0]) % 4 * 8 + col], xc_peer(d))
        px[p, col] = pmine[p]

    panel_near(0)
    for s, e in enumerate(RELAY):
        whole(relay_group(e), frelay.at[e % 8]).wait_recv()
        fpass[s] = fmask[e % NZ] + frelay[e % 8]
        put(17, fpass.at[s], fz.at[s], z_peer(e))
    for s, d in enumerate(NEAR):
        put(1, pown.at[1], pz.at[1, s], z_peer(d))

    panel_sum(0)
    whole(17, fz).wait_recv()
    fmine[...] = fmask[0] + jnp.sum(fz[...], axis=0)
    for d in XC_OFFS:
        put(7, fmine, fx.at[(4 - d[0]) % 4 * 8 + col], xc_peer(d))
    fx[col] = fmine[...]
    whole(3, dg.at[pl.ds(0, 3)]).wait_recv()
    for d in range(4):
        index = (y + d) % NY * NC + k
        put(18, dg.at[index], dg.at[index], c_peer((0, 1)))
    panel_near(1)
    whole(4, mx).wait_recv()
    mmine[...] = summed[pl.ds(x * NZ, NZ)] + mx[0] + mx[1] + mx[2]
    for s, d in enumerate(Z_OFFS):
        put(8, mmine.at[(z + d) % NZ], mz.at[s], z_peer(d))

    def panel_state(p):
        whole(5 + p, px.at[p, pl.ds(0, 31)]).wait_recv()
        value = px[p, 0:8] + px[p, 8:16] + px[p, 16:24] + px[p, 24:32]
        xs[p] = value.reshape(64, 128)
        return jnp.concatenate(
            [jnp.concatenate([xs[p, pl.ds(kk * 4 + b, 8, stride=8), :] for kk in range(2)], axis=0) for b in range(4)],
            axis=1,
        )

    eye = (
        lax.broadcasted_iota(jnp.int32, (64, 512), 1) == lax.broadcasted_iota(jnp.int32, (64, 512), 0) + col * 64
    ).astype(F32)
    w_first = (eye * is_first - fac[0].astype(F32) * other).astype(BF16)

    state = stacked(panel_state(0))
    whole(18, dg.at[pl.ds(0, 4)]).wait_recv()
    group = folded(dot_t(state, dg[...].reshape(128, 512).astype(BF16)))
    panel_sum(1)
    gather(MIDDLE)
    whole(7, fx.at[pl.ds(0, 31)]).wait_recv()
    piece = (fx[0:8] + fx[8:16] + fx[16:24] + fx[24:32]).reshape(128, 128).astype(BF16)
    tz[z] = folded(dot(stacked(group), piece))
    for d in Z_OFFS:
        put(9, tz.at[z], tz.at[z], z_peer(d))
    gather(LATE)

    solved = folded(dot_t(state, diag[0]))
    partial = folded(dot(stacked(solved), w_first))
    whole(8, mz).wait_recv()
    assembled = (mmine[z] + jnp.sum(mz[...], axis=0)) * other
    mine = lax.broadcasted_iota(jnp.int32, (8, 128), 0) == col
    placed = jnp.concatenate(
        [
            jnp.concatenate(
                [jnp.where(mine, assembled[kk * 4 + b:kk * 4 + b + 1, :], 0.0) for kk in range(2)], axis=0
            )
            for b in range(4)
        ],
        axis=1,
    )
    part[...] = partial + placed
    put(10, part, pair, c_peer((0, 1)))
    forward(EARLY)
    whole(10, pair).wait_recv()
    whole(10, pair).wait_send()
    part[...] = part[...] + pair[...]
    for s, d in enumerate((2, 1, 3)):
        put(11, part, pr.at[s], c_peer((d, 0)))
    state = panel_state(1)
    forward(MIDDLE)
    whole(11, pr).wait_recv()
    total = part[...] + jnp.sum(pr[...], axis=0)
    forward(LATE)
    for part_ in range(4):
        whole(30 + part_, halves(part_)).wait_recv()
    dhalf[...] = dfull[...].reshape(512, 512).T.astype(BF16)
    fhalf[...] = ffull[...].reshape(512, 512).astype(BF16)

    whole(9, tz.at[pl.ds(0, 15)]).wait_recv()
    update = jnp.concatenate([tz[b] + tz[4 + b] + tz[8 + b] + tz[12 + b] for b in range(4)], axis=1)
    solved = folded(dot(stacked(state - update), dhalf[...]))
    total = total + solved * is_second - folded(dot(stacked(solved), fhalf[...])) * other
    for b in range(4):
        for kk in range(2):
            order[b, pl.ds(kk, 8, stride=2), :] = total[kk * 8:kk * 8 + 8, b * 128:b * 128 + 128]
        lanes = slice(b * 128, b * 128 + 128)
        out[:, lanes] = order[b] + right[:, lanes] * other

    whole(0, pz.at[0]).wait_send()
    whole(1, pz.at[1]).wait_send()
    for e in RELAY:
        whole(relay_group(e), frelay.at[e % 8]).wait_send()
    whole(15, pfar.at[0]).wait_send()
    whole(16, pfar.at[1]).wait_send()
    whole(17, fz).wait_send()
    whole(3, dg.at[pl.ds(0, 3)]).wait_send()
    whole(18, dg.at[pl.ds(0, 4)]).wait_send()
    whole(4, mx).wait_send()
    whole(5, px.at[0, pl.ds(0, 31)]).wait_send()
    whole(6, px.at[1, pl.ds(0, 31)]).wait_send()
    whole(7, fx.at[pl.ds(0, 31)]).wait_send()
    whole(8, mz).wait_send()
    whole(9, tz.at[pl.ds(0, 15)]).wait_send()
    whole(11, pr).wait_send()
    for part_ in range(4):
        whole(26 + part_, three(part_)).wait_send()
        whole(30 + part_, halves(part_)).wait_send()


def body(right_side, child_updates, child_device, child_block, owners, diag_inverse, panel_factor):
    return pl.pallas_call(
        kernel,
        out_shape=jax.ShapeDtypeStruct((16, 512), F32),
        in_specs=[pl.BlockSpec(memory_space=pltpu.HBM)] * 7,
        out_specs=pl.BlockSpec(memory_space=pltpu.VMEM),
        scratch_shapes=[
            pltpu.SMEM((2,), jnp.int32),
            pltpu.VMEM((16, 512), F32),
            pltpu.VMEM((256, 2, 128), F32),
            pltpu.VMEM((1, 256), jnp.int32),
            pltpu.VMEM((1, 256), jnp.int32),
            pltpu.VMEM((2, 64, 512), BF16),
            pltpu.VMEM((2, 64, 512), BF16),
            pltpu.SemaphoreType.DMA((8,)),
            pltpu.VMEM((64, 8, 128), F32),
            pltpu.VMEM((16, 16, 128), F32),
            pltpu.VMEM((8, 16, 128), F32),
            pltpu.VMEM((16, 128), F32),
            pltpu.VMEM((32, 16, 128), F32),
            pltpu.VMEM((2, 8, 128), F32),
            pltpu.VMEM((2, 8, 8, 128), F32),
            pltpu.VMEM((2, 8, 128), F32),
            pltpu.VMEM((2, 32, 8, 128), F32),
            pltpu.VMEM((8, 16, 512), F32),
            pltpu.VMEM((3, 16, 8, 128), F32),
            pltpu.VMEM((16, 8, 128), F32),
            pltpu.VMEM((15, 8, 128), F32),
            pltpu.VMEM((16, 16, 128), F32),
            pltpu.VMEM((16, 512), F32),
            pltpu.VMEM((3, 16, 512), F32),
            pltpu.VMEM((16, 512), F32),
            pltpu.VMEM((2, 64, 128), F32),
            pltpu.VMEM((8, 128), F32),
            pltpu.VMEM((4, 16, 128), F32),
            pltpu.VMEM((8, 64, 512), F32),
            pltpu.VMEM((8, 64, 512), F32),
            pltpu.VMEM((512, 512), BF16),
            pltpu.VMEM((512, 512), BF16),
            pltpu.VMEM((2, 2, 8, 128), F32),
            pltpu.VMEM((2, 2, 8, 128), F32),
            pltpu.VMEM((8, 16, 128), F32),
            pltpu.VMEM((7, 16, 128), F32),
            pltpu.SemaphoreType.DMA((34,)),
            pltpu.SemaphoreType.DMA((34,)),
        ],
        compiler_params=pltpu.CompilerParams(
            collective_id=0, has_side_effects=True, vmem_limit_bytes=60 * 1024 * 1024
        ),
    )(
        owners, right_side, child_updates, child_device.reshape(1, 256), child_block.reshape(1, 256),
        diag_inverse, panel_factor,
    )


def solution(mesh):
    return jax.shard_map(
        body,
        mesh=mesh,
        in_specs=(
            P(None, "rows"),
            P("rows", "cols", None),
            P("rows", None),
            P("rows", None),
            P(),
            P(None, "cols", None),
            P(None, "cols", "rows"),
        ),
        out_specs=P(None, "rows"),
        check_vma=False,
    )
```
